128 devices in a mesh: node: 16 (over y_hi, z, core), local: 8 (over x, y_lo).
Axes of the slice: x: 4, y: 4 (y_hi: 2, y_lo: 2; y = y_hi * 2 + y_lo), z: 4, core: 2. Of those that a mesh axis runs over, the one named last changes fastest.
Arguments:
- heads_out: bfloat16 [16384, 4096], P(('node', 'local')), may hold values from -24 to 24
- residual: bfloat16 [16384, 8192], P(('node', 'local')), may hold values from -6 to 6
- out_proj: bfloat16 [4096, 8192], P('node', 'local'), may hold values from -0.09375 to 0.09375
- cotangent: bfloat16 [16384, 8192], P(('node', 'local')), may hold values from -24 to 24
Outputs:
- layer_out: bfloat16 [16384, 8192], P(('node', 'local'))
- grad_heads: bfloat16 [16384, 4096], P(('node', 'local'))
- grad_proj: bfloat16 [4096, 8192], P('node', 'local')
The draws below stay inside these ranges and needn't reach their ends.
All inputs are finite; a program needn't handle non-finite values.
Results may differ from the reference program's by a relative error of at most 0.025.
Values may be sent and summed in bfloat16 or wider, within the bound.
No kernel may reach another device: no remote copies, remote signals or barrier semaphores. Data moves between devices by JAX's collectives and lax.ppermute only.
A program may use at most 128 MiB of HBM per device.

```python
import jax
import jax.numpy as jnp
from jax import lax

D = 8192
A = 4096
TOKENS = 16384
N_NODE = 16
N_LOCAL = 8


def strengthened(values, own_key, source, target, shards_of, factor):
    owner, partner = [(jnp.arange(values.shape[position]) // (values.shape[position] // shards_of)).reshape([-1 if axis == position else 1 for axis in range(values.ndim)]) for position in (source, target)]
    chosen = jax.random.permutation(own_key, shards_of)[partner]
    strong = (owner == chosen) | (owner == (partner + shards_of // 2) % shards_of)
    return jnp.where(strong, factor * values, values)


def steps_of(own_key, shape, split, low, largest):
    factor_of, own = 1.0, jax.random.fold_in(own_key, 6)
    for axis_at, parts in split:
        draws = jnp.exp(jax.random.uniform(jax.random.fold_in(own, axis_at), (parts,), jnp.float32, low / len(split), largest / len(split)))
        factor_of = factor_of * jnp.repeat(draws, shape[axis_at] // parts).reshape([-1 if axis == axis_at else 1 for axis in range(len(shape))])
    return factor_of


def gaussian(rng, dims, scale, bound, split=(), kind=jnp.bfloat16):
    loudness = steps_of(rng, dims, split, -0.22, 0.18) if split else 1.0
    result = jax.random.normal(rng, dims, jnp.float32) * scale * loudness
    return jnp.minimum(jnp.maximum(result, -bound), bound).astype(kind)


def noise_with(own_key, shape, spread, reach, pieces, heavy, kind=jnp.bfloat16):
    array = spread * jax.random.normal(own_key, shape, jnp.float32)
    if pieces:
        array = array * steps_of(own_key, shape, pieces, -0.22, 0.18)
    return jnp.clip(strengthened(array, jax.random.fold_in(own_key, 3), *heavy), -reach, reach).astype(kind)


def setup_inputs(seed: int = 0) -> dict:
    streams_of = jax.random.split(jax.random.key(seed), 5)
    return {
        "heads_out": noise_with(streams_of[0], (TOKENS, A), 1.0, 24.0, ((0, 128),), (0, 1, 128, 5.5)),
        "residual": gaussian(streams_of[1], (TOKENS, D), 1.0, 6.0, ((0, 128),)),
        "out_proj": gaussian(streams_of[2], (A, D), A ** -0.5, 0.09375, ((0, 16), (1, 8))),
        "cotangent": noise_with(streams_of[3], (TOKENS, D), 1.0, 24.0, ((0, 128),), (0, 1, 128, 5.5)),
    }


def reference(heads_out, residual, out_proj, cotangent):
    projected = jnp.dot(heads_out, out_proj, preferred_element_type=jnp.float32).astype(jnp.bfloat16)
    projected = lax.optimization_barrier(projected)
    layer_out = (residual.astype(jnp.float32) + projected.astype(jnp.float32)).astype(jnp.bfloat16)
    width = D // N_LOCAL

    def act_block(carry, index):
        offset = (index * width).astype(jnp.int32)
        cot_block = lax.dynamic_slice_in_dim(cotangent, offset, width, 1)
        proj_block = lax.dynamic_slice_in_dim(out_proj, offset, width, 1)
        term = lax.dot_general(cot_block, proj_block, (((1,), (1,)), ((), ())), preferred_element_type=jnp.float32)
        term = lax.optimization_barrier(term.astype(jnp.bfloat16))
        return (carry + term.astype(jnp.float32), None)
    grad_heads, _ = lax.scan(act_block, jnp.zeros((TOKENS, A), jnp.float32), jnp.arange(N_LOCAL, dtype=jnp.int32))
    group = TOKENS // N_NODE
    factor = 1.0 / jnp.sqrt(jnp.float32(TOKENS))

    def weight_block(carry, index):
        offset = (index * group).astype(jnp.int32)
        feature_block = lax.dynamic_slice_in_dim(heads_out, offset, group, 0)
        cot_block = lax.dynamic_slice_in_dim(cotangent, offset, group, 0)
        term = lax.dot_general(feature_block, cot_block, (((0,), (0,)), ((), ())), preferred_element_type=jnp.float32) * factor
        term = lax.optimization_barrier(term.astype(jnp.bfloat16))
        return (carry + term.astype(jnp.float32), None)
    grad_proj, _ = lax.scan(weight_block, jnp.zeros((A, D), jnp.float32), jnp.arange(N_NODE, dtype=jnp.int32))
    return (layer_out, grad_heads.astype(jnp.bfloat16), grad_proj.astype(jnp.bfloat16))
```

```python
import jax
import jax.numpy as jnp
from jax import lax
from jax.sharding import Mesh, PartitionSpec as P

AXES = ("yh", "z", "c", "x", "yl")
GROUP = ("x", "c")
ROWS = ("yh", "z", "yl")


def swap(block):
    pairs = []
    for yh in range(2):
        for z in range(4):
            for c in range(2):
                for x in range(4):
                    for yl in range(2):
                        here = (((yh * 4 + z) * 2 + c) * 4 + x) * 2 + yl
                        there = (((yh * 4 + z) * 2 + yl) * 4 + x) * 2 + c
                        pairs.append((here, there))
    return lax.ppermute(block, AXES, pairs)


def per_device(heads_out, residual, out_proj, cotangent):
    heads = lax.all_gather(heads_out, GROUP, axis=0, tiled=True)
    proj = lax.all_gather(swap(out_proj), ROWS, axis=0, tiled=True)
    cot = lax.all_to_all(cotangent, GROUP, split_axis=1, concat_axis=0, tiled=True)
    factor = 1.0 / jnp.sqrt(jnp.float32(heads.shape[0] * lax.axis_size(ROWS)))
    product = lax.dot_general(heads, cot, (((0,), (0,)), ((), ())), preferred_element_type=jnp.float32)
    grad_proj = swap(
        lax.psum_scatter((product * factor).astype(jnp.bfloat16), ROWS, scatter_dimension=0, tiled=True)
    )
    act = lax.dot_general(cot, proj, (((1,), (1,)), ((), ())), preferred_element_type=jnp.float32)
    grad_heads = lax.psum_scatter(act.astype(jnp.bfloat16), GROUP, scatter_dimension=0, tiled=True)
    projected = jnp.dot(heads, proj, preferred_element_type=jnp.float32).astype(jnp.bfloat16)
    token_proj = lax.all_to_all(projected, GROUP, split_axis=0, concat_axis=1, tiled=True)
    layer_out = (residual.astype(jnp.float32) + token_proj.astype(jnp.float32)).astype(jnp.bfloat16)
    return (layer_out, grad_heads, grad_proj)


def solution(mesh):
    fine = Mesh(mesh.devices.reshape(2, 4, 2, 4, 2), AXES)
    tokens, grid = P(AXES, None), P(("yh", "z", "c"), ("x", "yl"))
    return jax.shard_map(
        per_device,
        mesh=fine,
        in_specs=(tokens, tokens, grid, tokens),
        out_specs=(tokens, tokens, grid),
        check_vma=False,
    )
```

```python
import functools

import jax
import jax.numpy as jnp
from jax import lax
from jax.experimental import pallas as pl
from jax.experimental.pallas import tpu as pltpu
from jax.sharding import Mesh, PartitionSpec as P

AXES = ("yh", "z", "c", "x", "yl")
BF16, F32 = jnp.bfloat16, jnp.float32


def flat(x, y, z, c):
    return ((((y // 2) * 4 + z) * 2 + c) * 4 + x) * 2 + y % 2


def moves(to):
    pairs = []
    for x in range(4):
        for y in range(4):
            for z in range(4):
                for c in range(2):
                    pairs.append((flat(x, y, z, c), flat(*to(x, y, z, c))))
    return sorted(pairs)


XP = moves(lambda x, y, z, c: ((x + 1) % 4, y, z, c))
XM = moves(lambda x, y, z, c: ((x + 3) % 4, y, z, c))
XX = moves(lambda x, y, z, c: ((x + 2) % 4, y, z, c))
YP = moves(lambda x, y, z, c: (x, (y + 1) % 4, z, c))
YM = moves(lambda x, y, z, c: (x, (y + 3) % 4, z, c))
ZP = moves(lambda x, y, z, c: (x, y, (z + 1) % 4, c))
ZM = moves(lambda x, y, z, c: (x, y, (z + 3) % 4, c))
CORE = moves(lambda x, y, z, c: (x, y, z, 1 - c))
SWAP = moves(lambda x, y, z, c: (x, y - y % 2 + c, z, y % 2))


def send(value, pairs):
    return lax.ppermute(value, AXES, pairs)


def gather(own, plus, minus):
    half = own.shape[0] // 2
    one = send(own, plus)
    three = send(own, minus)
    two_a = send(one[:half], plus)
    two_b = send(three[half:], minus)
    return own, one, two_a, two_b, three


def scatter(blocks, plus, minus):
    zero, one, two, three = blocks
    half = two.shape[0] // 2
    a = send(two[:half], minus)
    b = send(two[half:], plus)
    one = jnp.concatenate([add(one[:half], a), one[half:]])
    three = jnp.concatenate([three[:half], add(three[half:], b)])
    return zero, send(one, minus), send(three, plus)


def add(*terms):
    return functools.reduce(lambda p, q: p + q, [t.astype(F32) for t in terms]).astype(BF16)


def feature_block(k, y, z):
    first, second = (k % 16) // 4, k % 4
    dy = second if k < 16 else first
    dz = first if k < 16 else second
    yy, zz = (y + 4 - dy) % 4, (z + 4 - dz) % 4
    return (yy // 2) * 16 + zz * 4 + (yy % 2) * 2 + k // 16


def ordered_kernel(place, heads, out):
    for k in range(32):
        at = pl.multiple_of(feature_block(k, place[1], place[2]) * 128, 128)
        out[:, k * 128 : (k + 1) * 128] = heads[:, pl.ds(at, 128)]


def grad_heads_kernel(place, zero, one, three, out):
    for k in range(32):
        at = pl.multiple_of(feature_block(k, place[1], place[2]) * 128, 128)
        here = slice(k * 128, (k + 1) * 128)
        total = zero[:, here].astype(F32) + one[:, here].astype(F32) + three[:, here].astype(F32)
        out[:, pl.ds(at, 128)] = total.astype(BF16)


def layer_kernel(place, residual, zero, one, two, three, out):
    for d, piece in enumerate((zero, one, two, three)):
        xx = (place[0] + d) % 4
        for e in range(2):
            cc = (place[3] + e) % 2
            at = pl.multiple_of((xx * 2 + cc) * 1024, 1024)
            total = residual[:, pl.ds(at, 1024)].astype(F32) + piece[e].astype(F32)
            out[:, pl.ds(at, 1024)] = total.astype(BF16)


def local(kernel, shape, place, *operands):
    return pl.pallas_call(
        kernel,
        out_shape=jax.ShapeDtypeStruct(shape, BF16),
        in_specs=[pl.BlockSpec(memory_space=pltpu.SMEM)]
        + [pl.BlockSpec(memory_space=pltpu.VMEM)] * len(operands),
        out_specs=pl.BlockSpec(memory_space=pltpu.VMEM),
        compiler_params=pltpu.CompilerParams(vmem_limit_bytes=24 * 1024 * 1024),
    )(place, *operands)


def dot(a, b, dims):
    return lax.dot_general(a, b, (dims, ((), ())), preferred_element_type=F32)


def per_device(heads_out, residual, out_proj, cotangent):
    x, c = lax.axis_index("x"), lax.axis_index("c")
    y, z = 2 * lax.axis_index("yh") + lax.axis_index("yl"), lax.axis_index("z")
    place = jnp.stack([x, y, z, c]).astype(jnp.int32)
    rows = heads_out.shape[0]

    def columns(d, cc):
        return lax.dynamic_slice_in_dim(cotangent, ((x + d) % 4 * 2 + cc) * 1024, 1024, 1)

    given = jnp.concatenate([columns(d, 1 - c) for d in range(4)])
    swapped = send(out_proj, SWAP)
    got = send(given, CORE)
    message = [jnp.concatenate([columns(d, c), got[d * rows : (d + 1) * rows]]) for d in range(4)]
    arrived = [message[0], send(message[1], XP), send(message[2], XX), send(message[3], XM)]
    cot_own = jnp.concatenate([m[:rows] for m in arrived])
    cot_other = jnp.concatenate([m[rows:] for m in arrived])

    half = swapped.shape[0] // 2
    first = jnp.concatenate(gather(swapped[:half], YP, YM))
    second = jnp.concatenate(gather(swapped[half:], ZP, ZM))
    proj = jnp.concatenate(gather(first, ZP, ZM) + gather(second, YP, YM))

    ordered = local(ordered_kernel, heads_out.shape, place, heads_out)
    pieces = gather(ordered, XP, XM)
    heads_own = jnp.concatenate(pieces)
    heads_other = jnp.concatenate([send(p, CORE) for p in pieces])

    act_other = dot(cot_other, proj, ((1,), (1,))).astype(BF16)
    act_back = send(act_other, CORE)
    act = (dot(cot_own, proj, ((1,), (1,))) + act_back.astype(F32)).astype(BF16)
    parts = scatter([act[d * rows : (d + 1) * rows] for d in range(4)], XP, XM)
    grad_heads = local(grad_heads_kernel, heads_out.shape, place, *parts)

    factor = 1.0 / jnp.sqrt(jnp.float32(rows * 128))

    def weight(k):
        at = slice(k * 512, (k + 1) * 512)
        total = dot(heads_own[:, at], cot_own, ((0,), (0,))) + dot(heads_other[:, at], cot_other, ((0,), (0,)))
        return (total * factor).astype(BF16)

    def ring_sum(blocks, plus, minus):
        return add(*scatter(blocks, plus, minus))

    def split(block):
        n = block.shape[0] // 4
        return [block[d * n : (d + 1) * n] for d in range(4)]

    upper = ring_sum([weight(d) for d in range(4)], ZP, ZM)
    lower = ring_sum([weight(4 + d) for d in range(4)], YP, YM)
    upper = ring_sum(split(upper), YP, YM)
    lower = ring_sum(split(lower), ZP, ZM)
    grad_proj = send(jnp.concatenate([upper, lower]), SWAP)

    out_other = dot(heads_other, proj, ((1,), (0,))).astype(BF16)
    out_back = send(out_other, CORE)
    out_own = dot(heads_own, proj, ((1,), (0,))).astype(BF16)
    outgoing = [jnp.stack([out_own[d * rows : (d + 1) * rows], out_back[d * rows : (d + 1) * rows]]) for d in range(4)]
    incoming = [outgoing[0], send(outgoing[1], XM), send(outgoing[2], XX), send(outgoing[3], XP)]
    layer_out = local(layer_kernel, residual.shape, place, residual, *incoming)
    return (layer_out, grad_heads, grad_proj)


def solution(mesh):
    fine = Mesh(mesh.devices.reshape(2, 4, 2, 4, 2), AXES)
    tokens, grid = P(AXES, None), P(("yh", "z", "c"), ("x", "yl"))
    return jax.shard_map(
        per_device,
        mesh=fine,
        in_specs=(tokens, tokens, grid, tokens),
        out_specs=(tokens, tokens, grid),
        check_vma=False,
    )
```

```python
import functools

import jax
import jax.numpy as jnp
from jax import lax
from jax.experimental import pallas as pl
from jax.experimental.pallas import tpu as pltpu
from jax.sharding import Mesh, PartitionSpec as P

AXES = ("yh", "z", "c", "x", "yl")
BF16, F32 = jnp.bfloat16, jnp.float32
WIDE = 1024


def flat(x, y, z, c):
    return ((((y // 2) * 4 + z) * 2 + c) * 4 + x) * 2 + y % 2


def moves(to):
    pairs = []
    for x in range(4):
        for y in range(4):
            for z in range(4):
                for c in range(2):
                    pairs.append((flat(x, y, z, c), flat(*to(x, y, z, c))))
    return sorted(pairs)


X_AHEAD = moves(lambda x, y, z, c: ((x + 1 + 2 * c) % 4, y, z, c))
X_BACK = moves(lambda x, y, z, c: ((x + 3 + 2 * c) % 4, y, z, c))
Y_AHEAD = moves(lambda x, y, z, c: (x, (y + 1 + 2 * c) % 4, z, c))
Y_BACK = moves(lambda x, y, z, c: (x, (y + 3 + 2 * c) % 4, z, c))
Z_AHEAD = moves(lambda x, y, z, c: (x, y, (z + 1 + 2 * c) % 4, c))
Z_BACK = moves(lambda x, y, z, c: (x, y, (z + 3 + 2 * c) % 4, c))
X_ACROSS = moves(lambda x, y, z, c: ((x + 2) % 4, y, z, c))
CORE = moves(lambda x, y, z, c: (x, y, z, 1 - c))
SWAP = moves(lambda x, y, z, c: (x, y - y % 2 + c, z, y % 2))


def add(*terms):
    return functools.reduce(lambda p, q: p + q, [t.astype(F32) for t in terms]).astype(BF16)


def feature_block(k, y, z):
    part, far = k // 16, (k % 16) // 4
    dy, dz = (k % 4, far) if part == 0 else (far, k % 4)
    yy, zz = (y + 4 - dy) % 4, (z + 4 - dz) % 4
    return (yy // 2) * 16 + zz * 4 + (yy % 2) * 2 + part


def ordered_kernel(place, heads, out):
    for k in range(32):
        at = pl.multiple_of(feature_block(k, place[1], place[2]) * 128, 128)
        out[:, k * 128 : (k + 1) * 128] = heads[:, pl.ds(at, 128)]


def restored_kernel(place, grad, out):
    for k in range(32):
        at = pl.multiple_of(feature_block(k, place[1], place[2]) * 128, 128)
        out[:, pl.ds(at, 128)] = grad[:, k * 128 : (k + 1) * 128]


def columns_kernel(place, cotangent, here, ahead, back, across):
    x, c = place[0], place[3]
    step = 1 + 2 * c
    for distance, out in ((0, here), (step, ahead), (4 - step, back), (2, across)):
        for e in range(2):
            at = pl.multiple_of(((x + distance) % 4 * 2 + (c + e) % 2) * WIDE, WIDE)
            out[e] = cotangent[:, pl.ds(at, WIDE)]


def tokens_kernel(place, here, ahead, back, across, given, out):
    x, c = place[0], place[3]
    step = 1 + 2 * c
    n = here.shape[1]
    for e, (distance, piece) in enumerate(((0, here), (4 - step, ahead), (2, across), (step, back))):
        at = (x + distance) % 4 * 2
        out[pl.ds(pl.multiple_of((at + c) * n, n), n), :] = piece[0]
    for e, distance in enumerate((0, step, 2, 4 - step)):
        at = (x + distance) % 4 * 2
        out[pl.ds(pl.multiple_of((at + 1 - c) * n, n), n), :] = given[e * n : (e + 1) * n, :]


def outgoing_kernel(place, own, got, here, ahead, back, across):
    x, c = place[0], place[3]
    step = 1 + 2 * c
    for distance, out in ((0, here), (step, ahead), (4 - step, back), (2, across)):
        out[0] = own[(x + distance) % 4]
        out[1] = got[(x + distance) % 4]


def layer_kernel(place, residual, here, ahead, back, across, out):
    x, c = place[0], place[3]
    step = 1 + 2 * c
    pieces = []
    for distance, both in ((0, here), (4 - step, ahead), (step, back), (2, across)):
        pieces += [(x + distance, c, both.at[0]), (x + distance, 1 - c, both.at[1])]
    for xx, cc, piece in pieces:
        at = pl.multiple_of((xx % 4 * 2 + cc) * WIDE, WIDE)
        total = residual[:, pl.ds(at, WIDE)].astype(F32) + piece[...].astype(F32)
        out[:, pl.ds(at, WIDE)] = total.astype(BF16)


def local(kernel, shapes, place, *operands):
    vmem = pl.BlockSpec(memory_space=pltpu.VMEM)
    return pl.pallas_call(
        kernel,
        out_shape=jax.tree.map(lambda s: jax.ShapeDtypeStruct(s, BF16), shapes, is_leaf=lambda s: isinstance(s[0], int)),
        in_specs=[pl.BlockSpec(memory_space=pltpu.SMEM)] + [vmem] * len(operands),
        out_specs=jax.tree.map(lambda s: vmem, shapes, is_leaf=lambda s: isinstance(s[0], int)),
        compiler_params=pltpu.CompilerParams(vmem_limit_bytes=24 * 1024 * 1024),
    )(place, *operands)


def dot(a, b, dims):
    return lax.dot_general(a, b, (dims, ((), ())), preferred_element_type=F32)


class Line:
    def __init__(self):
        self.token = jnp.zeros((), jnp.int32)

    def wait(self, *values):
        self.token, *values = lax.optimization_barrier((self.token, *values))
        return values[0] if len(values) == 1 else values

    def send(self, value, pairs):
        return lax.ppermute(self.wait(value), AXES, pairs)


def per_device(heads_out, residual, out_proj, cotangent):
    x, c = lax.axis_index("x"), lax.axis_index("c")
    y, z = 2 * lax.axis_index("yh") + lax.axis_index("yl"), lax.axis_index("z")
    place = jnp.stack([x, y, z, c]).astype(jnp.int32)
    first = c == 0
    n = heads_out.shape[0]
    line = Line()
    send, wait = line.send, line.wait

    def pick(ahead, back):
        return jnp.where(first, ahead, back), jnp.where(first, back, ahead)

    def ring(zero, ahead, far, back):
        one, three = pick(ahead, back)
        return jnp.concatenate([zero, one, far, three])

    mine = send(out_proj, SWAP)
    ordered = local(ordered_kernel, heads_out.shape, place, heads_out)
    heads = lax.all_gather(ordered, ("x", "c"), axis=0, tiled=True)
    pair = (2, n, WIDE)
    cot_here, ahead, back, across = local(columns_kernel, (pair, pair, pair, pair), place, cotangent)
    cot_ahead = send(ahead, X_AHEAD)
    cot_back = send(back, X_BACK)
    cot_across = send(across, X_ACROSS)
    mine = wait(mine)
    half = mine.shape[0] // 2
    up, lo = mine[:half], mine[half:]
    up_ahead = send(up, Y_AHEAD)
    lo_ahead = send(lo, Z_AHEAD)
    up_ahead = wait(up_ahead)
    up_back = send(up, Y_BACK)
    lo_ahead = wait(lo_ahead)
    lo_back = send(lo, Z_BACK)
    cot_ahead = wait(cot_ahead)
    up_far = send(up_ahead, Y_AHEAD)
    cot_back = wait(cot_back)
    lo_far = send(lo_ahead, Z_AHEAD)
    up_back, up_far = wait(up_back, up_far)
    up = ring(up, up_ahead, up_far, up_back)
    up_ahead = send(up, Z_AHEAD)
    lo_back, lo_far = wait(lo_back, lo_far)
    lo = ring(lo, lo_ahead, lo_far, lo_back)
    lo_ahead = send(lo, Y_AHEAD)
    up_back = send(up, Z_BACK)
    lo_back = send(lo, Y_BACK)
    cot_across = wait(cot_across)
    cot_given = send(jnp.concatenate([cot_here[1], cot_ahead[1], cot_across[1], cot_back[1]]), CORE)
    cot_given = wait(cot_given)
    cot = local(
        tokens_kernel, (8 * n, WIDE), place, cot_here, cot_ahead, cot_back, cot_across, cot_given
    )
    up_ahead = wait(up_ahead)
    up_far = send(up_ahead, Z_AHEAD)
    lo_ahead = wait(lo_ahead)
    lo_far = send(lo_ahead, Y_AHEAD)
    up_back, lo_back = wait(up_back, lo_back)

    heads = wait(heads)
    factor = 1.0 / jnp.sqrt(jnp.float32(n * 128))

    def weight(k):
        return (dot(lax.dynamic_slice_in_dim(heads, k * 512, 512, 1), cot, ((0,), (0,))) * factor).astype(BF16)

    def row(block, d):
        m = block.shape[0] // 4
        return block[d * m : (d + 1) * m]

    one, three = jnp.where(first, 1, 3), jnp.where(first, 3, 1)
    sum_up_far = send(weight(2), Z_BACK)
    sum_lo_far = send(weight(6), Y_BACK)
    up_far, lo_far = wait(up_far, lo_far)
    sum_up_back = send(weight(three), Z_AHEAD)
    sum_lo_back = send(weight(4 + three), Y_AHEAD)
    proj = jnp.concatenate([ring(up, up_ahead, up_far, up_back), ring(lo, lo_ahead, lo_far, lo_back)])
    act = dot(cot, proj, ((1,), (1,))).astype(BF16)
    act = wait(act)
    grad_heads = lax.psum_scatter(act, ("x", "c"), scatter_dimension=0, tiled=True)
    weight_up, weight_lo = weight(one), weight(4 + one)
    sum_up_far = wait(sum_up_far)
    sum_up_ahead = send(add(weight_up, sum_up_far), Z_BACK)
    sum_lo_far = wait(sum_lo_far)
    sum_lo_ahead = send(add(weight_lo, sum_lo_far), Y_BACK)
    weight_up, weight_lo = wait(weight(0), weight(4))

    out = wait(dot(heads, proj, ((1,), (0,))).astype(BF16)).reshape(4, 2, n, WIDE)
    out_mine, out_given = [lax.dynamic_index_in_dim(out, e, 1, keepdims=False) for e in (c, 1 - c)]
    out_given = send(out_given, CORE)
    sum_up_back, sum_up_ahead = wait(sum_up_back, sum_up_ahead)
    up = add(weight_up, sum_up_ahead, sum_up_back)
    sum_up_far = send(row(up, 2), Y_BACK)
    sum_lo_back, sum_lo_ahead = wait(sum_lo_back, sum_lo_ahead)
    lo = add(weight_lo, sum_lo_ahead, sum_lo_back)
    sum_lo_far = send(row(lo, 2), Z_BACK)
    out_given = wait(out_given)
    out_here, ahead, back, across = local(outgoing_kernel, (pair, pair, pair, pair), place, out_mine, out_given)
    out_ahead = send(ahead, X_AHEAD)
    out_back = send(back, X_BACK)
    up_one, up_three = pick(row(up, 1), row(up, 3))
    lo_one, lo_three = pick(row(lo, 1), row(lo, 3))
    sum_up_back = send(up_three, Y_AHEAD)
    sum_up_far = wait(sum_up_far)
    sum_lo_back = send(lo_three, Z_AHEAD)
    sum_lo_far = wait(sum_lo_far)
    sum_up_ahead = send(add(up_one, sum_up_far), Y_BACK)
    sum_up_back = wait(sum_up_back)
    sum_lo_ahead = send(add(lo_one, sum_lo_far), Z_BACK)
    sum_lo_back = wait(sum_lo_back)
    out_across = send(across, X_ACROSS)
    sum_up_ahead, sum_lo_ahead = wait(sum_up_ahead, sum_lo_ahead)
    grad_proj = jnp.concatenate(
        [add(row(up, 0), sum_up_ahead, sum_up_back), add(row(lo, 0), sum_lo_ahead, sum_lo_back)]
    )
    grad_proj = send(grad_proj, SWAP)
    out_ahead, out_back, out_across = wait(out_ahead, out_back, out_across)
    layer_out = local(layer_kernel, residual.shape, place, residual, out_here, out_ahead, out_back, out_across)
    grad_heads = local(restored_kernel, heads_out.shape, place, grad_heads)
    return (layer_out, grad_heads, grad_proj)


def solution(mesh):
    fine = Mesh(mesh.devices.reshape(2, 4, 2, 4, 2), AXES)
    tokens, grid = P(AXES, None), P(("yh", "z", "c"), ("x", "yl"))
    return jax.shard_map(
        per_device,
        mesh=fine,
        in_specs=(tokens, tokens, grid, tokens),
        out_specs=(tokens, tokens, grid),
        check_vma=False,
    )
```

```python
import functools

import jax
import jax.numpy as jnp
from jax import lax
from jax.experimental import pallas as pl
from jax.experimental.pallas import tpu as pltpu
from jax.sharding import Mesh, PartitionSpec as P

AXES = ("yh", "z", "c", "x", "yl")
BF16, F32 = jnp.bfloat16, jnp.float32
WIDE = 1024


def flat(x, y, z, c):
    return ((((y // 2) * 4 + z) * 2 + c) * 4 + x) * 2 + y % 2


def moves(to):
    pairs = []
    for x in range(4):
        for y in range(4):
            for z in range(4):
                for c in range(2):
                    pairs.append((flat(x, y, z, c), flat(*to(x, y, z, c))))
    return sorted(pairs)


X_AHEAD = moves(lambda x, y, z, c: ((x + 1 + 2 * c) % 4, y, z, c))
X_BACK = moves(lambda x, y, z, c: ((x + 3 + 2 * c) % 4, y, z, c))
X_ACROSS = moves(lambda x, y, z, c: ((x + 2) % 4, y, z, c))
Y_AHEAD = moves(lambda x, y, z, c: (x, (y + 1 + 2 * c) % 4, z, c))
Y_BACK = moves(lambda x, y, z, c: (x, (y + 3 + 2 * c) % 4, z, c))
Z_AHEAD = moves(lambda x, y, z, c: (x, y, (z + 1 + 2 * c) % 4, c))
Z_BACK = moves(lambda x, y, z, c: (x, y, (z + 3 + 2 * c) % 4, c))
Y_ACROSS = moves(lambda x, y, z, c: (x, (y + 2) % 4, z, c))
Z_ACROSS = moves(lambda x, y, z, c: (x, y, (z + 2) % 4, c))
CORE = moves(lambda x, y, z, c: (x, y, z, 1 - c))
SWAP = moves(lambda x, y, z, c: (x, y - y % 2 + c, z, y % 2))


def add(*terms):
    return functools.reduce(lambda p, q: p + q, [t.astype(F32) for t in terms]).astype(BF16)


def feature_block(k, y, z):
    part, far = k // 16, (k % 16) // 4
    dy, dz = (k % 4, far) if part == 0 else (far, k % 4)
    yy, zz = (y + 4 - dy) % 4, (z + 4 - dz) % 4
    return (yy // 2) * 16 + zz * 4 + (yy % 2) * 2 + part


def ordered_kernel(place, heads, out):
    for k in range(32):
        at = pl.multiple_of(feature_block(k, place[1], place[2]) * 128, 128)
        out[:, k * 128 : (k + 1) * 128] = heads[:, pl.ds(at, 128)]


def restored_kernel(place, grad, out):
    for k in range(32):
        at = pl.multiple_of(feature_block(k, place[1], place[2]) * 128, 128)
        out[:, pl.ds(at, 128)] = grad[:, k * 128 : (k + 1) * 128]


def columns_kernel(place, cotangent, here, ahead, back, across):
    x, c = place[0], place[3]
    step = 1 + 2 * c
    for distance, out in ((0, here), (step, ahead), (4 - step, back), (2, across)):
        for e in range(2):
            at = pl.multiple_of(((x + distance) % 4 * 2 + (c + e) % 2) * WIDE, WIDE)
            out[e] = cotangent[:, pl.ds(at, WIDE)]


def tokens_kernel(place, here, ahead, back, across, given, out):
    x, c = place[0], place[3]
    step = 1 + 2 * c
    n = here.shape[1]
    for e, (distance, piece) in enumerate(((0, here), (4 - step, ahead), (2, across), (step, back))):
        at = (x + distance) % 4 * 2
        out[pl.ds(pl.multiple_of((at + c) * n, n), n), :] = piece[0]
    for e, distance in enumerate((0, step, 2, 4 - step)):
        at = (x + distance) % 4 * 2
        out[pl.ds(pl.multiple_of((at + 1 - c) * n, n), n), :] = given[e * n : (e + 1) * n, :]


def local(kernel, shapes, place, *operands):
    vmem = pl.BlockSpec(memory_space=pltpu.VMEM)
    return pl.pallas_call(
        kernel,
        out_shape=jax.tree.map(lambda s: jax.ShapeDtypeStruct(s, BF16), shapes, is_leaf=lambda s: isinstance(s[0], int)),
        in_specs=[pl.BlockSpec(memory_space=pltpu.SMEM)] + [vmem] * len(operands),
        out_specs=jax.tree.map(lambda s: vmem, shapes, is_leaf=lambda s: isinstance(s[0], int)),
        compiler_params=pltpu.CompilerParams(vmem_limit_bytes=8 * 1024 * 1024),
    )(place, *operands)


def after(value, *earlier):
    anywhere = pl.BlockSpec(memory_space=pl.ANY)
    return pl.pallas_call(
        lambda *refs: None,
        out_shape=jax.ShapeDtypeStruct(value.shape, value.dtype),
        in_specs=[anywhere] * (1 + len(earlier)),
        out_specs=anywhere,
        input_output_aliases={0: 0},
        compiler_params=pltpu.CompilerParams(vmem_limit_bytes=1024 * 1024),
    )(value, *earlier)


def dot(a, b, dims):
    return lax.dot_general(a, b, (dims, ((), ())), preferred_element_type=F32)


class Line:
    def __init__(self):
        self.token = jnp.zeros((), jnp.int32)

    def wait(self, *values):
        self.token, *values = lax.optimization_barrier((self.token, *values))
        return values[0] if len(values) == 1 else values

    def send(self, value, pairs):
        return lax.ppermute(self.wait(value), AXES, pairs)


def per_device(heads_out, residual, out_proj, cotangent):
    x, c = lax.axis_index("x"), lax.axis_index("c")
    y, z = 2 * lax.axis_index("yh") + lax.axis_index("yl"), lax.axis_index("z")
    place = jnp.stack([x, y, z, c]).astype(jnp.int32)
    first = c == 0
    n = heads_out.shape[0]
    line = Line()
    send, wait = line.send, line.wait

    def pick(ahead, back):
        return jnp.where(first, ahead, back), jnp.where(first, back, ahead)

    def ring(zero, ahead, far, back):
        one, three = pick(ahead, back)
        return jnp.concatenate([zero, one, far, three])

    mine = send(out_proj, SWAP)
    ordered = local(ordered_kernel, heads_out.shape, place, heads_out)
    heads = lax.all_gather(ordered, ("x", "c"), axis=0, tiled=True)
    pair = (2, n, WIDE)
    cot_here, ahead, back, across = local(columns_kernel, (pair, pair, pair, pair), place, cotangent)
    cot_ahead = send(ahead, X_AHEAD)
    mine = wait(mine)
    half = mine.shape[0] // 2
    up, lo = mine[:half], mine[half:]
    up_ahead = send(up, Y_AHEAD)
    lo_ahead = send(lo, Z_AHEAD)
    up_back = send(up, Y_BACK)
    lo_back = send(lo, Z_BACK)
    up_ahead = wait(up_ahead)
    up_far = send(up, Y_ACROSS)
    lo_ahead = wait(lo_ahead)
    lo_far = send(lo, Z_ACROSS)
    cot_ahead = wait(cot_ahead)
    cot_back = send(back, X_BACK)
    up_back, up_far = wait(up_back, up_far)
    up = ring(up, up_ahead, up_far, up_back)
    up_ahead = send(up, Z_AHEAD)
    lo_back, lo_far = wait(lo_back, lo_far)
    lo = ring(lo, lo_ahead, lo_far, lo_back)
    lo_ahead = send(lo, Y_AHEAD)
    up_back = send(up, Z_BACK)
    lo_back = send(lo, Y_BACK)
    cot_back = wait(cot_back)
    cot_across = send(across, X_ACROSS)
    up_ahead = wait(up_ahead)
    up_far = send(up_ahead, Z_AHEAD)
    lo_ahead = wait(lo_ahead)
    lo_far = send(lo_ahead, Y_AHEAD)
    cot_across = wait(cot_across)
    cot_given = send(jnp.concatenate([cot_here[1], cot_ahead[1], cot_across[1], cot_back[1]]), CORE)
    up_back, lo_back = wait(up_back, lo_back)
    cot_given = wait(cot_given)
    cot = local(tokens_kernel, (8 * n, WIDE), place, cot_here, cot_ahead, cot_back, cot_across, cot_given)

    heads = wait(heads)
    factor = 1.0 / jnp.sqrt(jnp.float32(n * 128))

    def weight(k):
        return (dot(lax.dynamic_slice_in_dim(heads, k * 512, 512, 1), cot, ((0,), (0,))) * factor).astype(BF16)

    def row(block, d):
        m = block.shape[0] // 4
        return block[d * m : (d + 1) * m]

    one, three = jnp.where(first, 1, 3), jnp.where(first, 3, 1)
    weight_up, weight_lo = weight(2), weight(6)
    sum_up_far = send(weight_up, Z_BACK)
    sum_lo_far = send(weight_lo, Y_BACK)
    started = [weight_up, weight_lo]
    up_far, lo_far = wait(up_far, lo_far)
    started += [weight(three), weight(4 + three)]
    sum_up_back = send(started[2], Z_AHEAD)
    sum_lo_back = send(started[3], Y_AHEAD)
    proj = jnp.concatenate([ring(up, up_ahead, up_far, up_back), ring(lo, lo_ahead, lo_far, lo_back)])
    act = dot(cot, proj, ((1,), (1,))).astype(BF16)
    act = wait(act)
    grad_heads = lax.psum_scatter(act, ("x", "c"), scatter_dimension=0, tiled=True)
    weight_up, weight_lo = weight(one), weight(4 + one)

    out = dot(heads, after(proj, act, *started), ((1,), (0,))).astype(BF16)
    token_proj = lax.all_to_all(out, ("x", "c"), split_axis=0, concat_axis=1, tiled=True)
    sum_up_far, sum_lo_far = after(sum_up_far, out), after(sum_lo_far, out)
    sum_up_ahead = send(add(weight_up, sum_up_far), Z_BACK)
    sum_lo_ahead = send(add(weight_lo, sum_lo_far), Y_BACK)
    weight_up, weight_lo = weight(0), weight(4)
    sum_up_back, sum_up_ahead = wait(sum_up_back, sum_up_ahead)
    up = add(weight_up, sum_up_ahead, sum_up_back)
    sum_up_far = send(row(up, 2), Y_BACK)
    sum_lo_back, sum_lo_ahead = wait(sum_lo_back, sum_lo_ahead)
    lo = add(weight_lo, sum_lo_ahead, sum_lo_back)
    sum_lo_far = send(row(lo, 2), Z_BACK)
    up_one, up_three = pick(row(up, 1), row(up, 3))
    lo_one, lo_three = pick(row(lo, 1), row(lo, 3))
    sum_up_back = send(up_three, Y_AHEAD)
    sum_up_far = wait(sum_up_far)
    sum_lo_back = send(lo_three, Z_AHEAD)
    sum_lo_far = wait(sum_lo_far)
    sum_up_ahead = send(add(up_one, sum_up_far), Y_BACK)
    sum_up_back = wait(sum_up_back)
    sum_lo_ahead = send(add(lo_one, sum_lo_far), Z_BACK)
    sum_lo_back = wait(sum_lo_back)
    sum_up_ahead, sum_lo_ahead = wait(sum_up_ahead, sum_lo_ahead)
    grad_proj = jnp.concatenate(
        [add(row(up, 0), sum_up_ahead, sum_up_back), add(row(lo, 0), sum_lo_ahead, sum_lo_back)]
    )
    grad_proj = send(grad_proj, SWAP)
    layer_out = add(residual, token_proj)
    grad_heads = local(restored_kernel, heads_out.shape, place, grad_heads)
    return (layer_out, grad_heads, grad_proj)


def solution(mesh):
    fine = Mesh(mesh.devices.reshape(2, 4, 2, 4, 2), AXES)
    tokens, grid = P(AXES, None), P(("yh", "z", "c"), ("x", "yl"))
    return jax.shard_map(
        per_device,
        mesh=fine,
        in_specs=(tokens, tokens, grid, tokens),
        out_specs=(tokens, tokens, grid),
        check_vma=False,
    )
```

```python
import functools

import jax
import jax.numpy as jnp
from jax import lax
from jax.experimental import pallas as pl
from jax.experimental.pallas import tpu as pltpu
from jax.sharding import Mesh, PartitionSpec as P

AXES = ("yh", "z", "c", "x", "yl")
BF16, F32 = jnp.bfloat16, jnp.float32
WIDE = 1024


def flat(x, y, z, c):
    return ((((y // 2) * 4 + z) * 2 + c) * 4 + x) * 2 + y % 2


def moves(to):
    pairs = []
    for x in range(4):
        for y in range(4):
            for z in range(4):
                for c in range(2):
                    pairs.append((flat(x, y, z, c), flat(*to(x, y, z, c))))
    return sorted(pairs)


X_AHEAD = moves(lambda x, y, z, c: ((x + 1 + 2 * c) % 4, y, z, c))
X_BACK = moves(lambda x, y, z, c: ((x + 3 + 2 * c) % 4, y, z, c))
X_ACROSS = moves(lambda x, y, z, c: ((x + 2) % 4, y, z, c))
Y_AHEAD = moves(lambda x, y, z, c: (x, (y + 1 + 2 * c) % 4, z, c))
Y_BACK = moves(lambda x, y, z, c: (x, (y + 3 + 2 * c) % 4, z, c))
Z_AHEAD = moves(lambda x, y, z, c: (x, y, (z + 1 + 2 * c) % 4, c))
Z_BACK = moves(lambda x, y, z, c: (x, y, (z + 3 + 2 * c) % 4, c))
Y_ACROSS = moves(lambda x, y, z, c: (x, (y + 2) % 4, z, c))
Z_ACROSS = moves(lambda x, y, z, c: (x, y, (z + 2) % 4, c))
CORE = moves(lambda x, y, z, c: (x, y, z, 1 - c))
SWAP = moves(lambda x, y, z, c: (x, y - y % 2 + c, z, y % 2))


def add(*terms):
    return functools.reduce(lambda p, q: p + q, [t.astype(F32) for t in terms]).astype(BF16)


def feature_block(k, y, z):
    part, far = k // 16, (k % 16) // 4
    dy, dz = (k % 4, far) if part == 0 else (far, k % 4)
    yy, zz = (y + 4 - dy) % 4, (z + 4 - dz) % 4
    return (yy // 2) * 16 + zz * 4 + (yy % 2) * 2 + part


def ordered_kernel(place, heads, out):
    for k in range(32):
        at = pl.multiple_of(feature_block(k, place[1], place[2]) * 128, 128)
        out[:, k * 128 : (k + 1) * 128] = heads[:, pl.ds(at, 128)]


def restored_kernel(place, grad, out):
    for k in range(32):
        at = pl.multiple_of(feature_block(k, place[1], place[2]) * 128, 128)
        out[:, pl.ds(at, 128)] = grad[:, k * 128 : (k + 1) * 128]


def columns_kernel(place, cotangent, here, ahead, back, across):
    x, c = place[0], place[3]
    step = 1 + 2 * c
    for distance, out in ((0, here), (step, ahead), (4 - step, back), (2, across)):
        for e in range(2):
            at = pl.multiple_of(((x + distance) % 4 * 2 + (c + e) % 2) * WIDE, WIDE)
            out[e] = cotangent[:, pl.ds(at, WIDE)]


def tokens_kernel(place, here, ahead, back, across, given, out):
    x, c = place[0], place[3]
    step = 1 + 2 * c
    n = here.shape[1]
    for e, (distance, piece) in enumerate(((0, here), (4 - step, ahead), (2, across), (step, back))):
        at = (x + distance) % 4 * 2
        out[pl.ds(pl.multiple_of((at + c) * n, n), n), :] = piece[0]
    for e, distance in enumerate((0, step, 2, 4 - step)):
        at = (x + distance) % 4 * 2
        out[pl.ds(pl.multiple_of((at + 1 - c) * n, n), n), :] = given[e * n : (e + 1) * n, :]


def local(kernel, shapes, place, *operands):
    vmem = pl.BlockSpec(memory_space=pltpu.VMEM)
    return pl.pallas_call(
        kernel,
        out_shape=jax.tree.map(lambda s: jax.ShapeDtypeStruct(s, BF16), shapes, is_leaf=lambda s: isinstance(s[0], int)),
        in_specs=[pl.BlockSpec(memory_space=pltpu.SMEM)] + [vmem] * len(operands),
        out_specs=jax.tree.map(lambda s: vmem, shapes, is_leaf=lambda s: isinstance(s[0], int)),
        compiler_params=pltpu.CompilerParams(vmem_limit_bytes=8 * 1024 * 1024),
    )(place, *operands)


def after(value, *earlier):
    anywhere = pl.BlockSpec(memory_space=pl.ANY)
    return pl.pallas_call(
        lambda *refs: None,
        out_shape=jax.ShapeDtypeStruct(value.shape, value.dtype),
        in_specs=[anywhere] * (1 + len(earlier)),
        out_specs=anywhere,
        input_output_aliases={0: 0},
        compiler_params=pltpu.CompilerParams(vmem_limit_bytes=1024 * 1024),
    )(value, *earlier)


def dot(a, b, dims):
    return lax.dot_general(a, b, (dims, ((), ())), preferred_element_type=F32)


class Line:
    def __init__(self):
        self.token = jnp.zeros((), jnp.int32)

    def wait(self, *values):
        self.token, *values = lax.optimization_barrier((self.token, *values))
        return values[0] if len(values) == 1 else values

    def send(self, value, pairs):
        return lax.ppermute(self.wait(value), AXES, pairs)


def per_device(heads_out, residual, out_proj, cotangent):
    x, c = lax.axis_index("x"), lax.axis_index("c")
    y, z = 2 * lax.axis_index("yh") + lax.axis_index("yl"), lax.axis_index("z")
    place = jnp.stack([x, y, z, c]).astype(jnp.int32)
    first = c == 0
    n = heads_out.shape[0]
    line = Line()
    send, wait = line.send, line.wait

    def pick(ahead, back):
        return jnp.where(first, ahead, back), jnp.where(first, back, ahead)

    def ring(zero, ahead, far, back):
        one, three = pick(ahead, back)
        return jnp.concatenate([zero, one, far, three])

    mine = send(out_proj, SWAP)
    ordered = local(ordered_kernel, heads_out.shape, place, heads_out)
    heads = lax.all_gather(ordered, ("x", "c"), axis=0, tiled=True)
    pair = (2, n, WIDE)
    cot_here, ahead, back, across = local(columns_kernel, (pair, pair, pair, pair), place, cotangent)
    cot_ahead = send(ahead, X_AHEAD)
    mine = wait(mine)
    half = mine.shape[0] // 2
    up, lo = mine[:half], mine[half:]
    up_ahead = send(up, Y_AHEAD)
    lo_ahead = send(lo, Z_AHEAD)
    up_back = send(up, Y_BACK)
    lo_back = send(lo, Z_BACK)
    up_ahead = wait(up_ahead)
    up_far = send(up, Y_ACROSS)
    lo_ahead = wait(lo_ahead)
    lo_far = send(lo, Z_ACROSS)
    cot_ahead = wait(cot_ahead)
    cot_back = send(back, X_BACK)
    up_back, up_far = wait(up_back, up_far)
    up = ring(up, up_ahead, up_far, up_back)
    up_ahead = send(up, Z_AHEAD)
    lo_back, lo_far = wait(lo_back, lo_far)
    lo = ring(lo, lo_ahead, lo_far, lo_back)
    lo_ahead = send(lo, Y_AHEAD)
    up_back = send(up, Z_BACK)
    lo_back = send(lo, Y_BACK)
    cot_back = wait(cot_back)
    cot_across = send(across, X_ACROSS)
    up_ahead = wait(up_ahead)
    up_far = send(up_ahead, Z_AHEAD)
    lo_ahead = wait(lo_ahead)
    lo_far = send(lo_ahead, Y_AHEAD)
    cot_across = wait(cot_across)
    cot_given = send(jnp.concatenate([cot_here[1], cot_ahead[1], cot_across[1], cot_back[1]]), CORE)
    up_back, lo_back = wait(up_back, lo_back)
    cot_given = wait(cot_given)
    cot = local(tokens_kernel, (8 * n, WIDE), place, cot_here, cot_ahead, cot_back, cot_across, cot_given)

    heads = wait(heads)
    factor = 1.0 / jnp.sqrt(jnp.float32(n * 128))

    def weight(k):
        return (dot(lax.dynamic_slice_in_dim(heads, k * 512, 512, 1), cot, ((0,), (0,))) * factor).astype(BF16)

    def row(block, d):
        m = block.shape[0] // 4
        return block[d * m : (d + 1) * m]

    one, three = jnp.where(first, 1, 3), jnp.where(first, 3, 1)
    weight_up, weight_lo = weight(2), weight(6)
    sum_up_far = send(weight_up, Z_BACK)
    sum_lo_far = send(weight_lo, Y_BACK)
    started = [weight_up, weight_lo]
    up_far, lo_far = wait(up_far, lo_far)
    started += [weight(three), weight(4 + three)]
    sum_up_back = send(started[2], Z_AHEAD)
    sum_lo_back = send(started[3], Y_AHEAD)
    proj = jnp.concatenate([ring(up, up_ahead, up_far, up_back), ring(lo, lo_ahead, lo_far, lo_back)])
    act = dot(cot, proj, ((1,), (1,))).astype(BF16)
    act = wait(act)
    grad_heads = lax.psum_scatter(act, ("x", "c"), scatter_dimension=0, tiled=True)
    weight_up, weight_lo = weight(one), weight(4 + one)

    out = dot(heads, after(proj, *started), ((1,), (0,))).astype(BF16)
    token_proj = lax.all_to_all(out, ("x", "c"), split_axis=0, concat_axis=1, tiled=True)
    sum_up_far, sum_lo_far = after(sum_up_far, out), after(sum_lo_far, out)
    sum_up_ahead = send(add(weight_up, sum_up_far), Z_BACK)
    sum_lo_ahead = send(add(weight_lo, sum_lo_far), Y_BACK)
    weight_up, weight_lo = weight(0), weight(4)
    sum_up_back, sum_up_ahead = wait(sum_up_back, sum_up_ahead)
    up = add(weight_up, sum_up_ahead, sum_up_back)
    sum_up_far = send(row(up, 2), Y_BACK)
    sum_lo_back, sum_lo_ahead = wait(sum_lo_back, sum_lo_ahead)
    lo = add(weight_lo, sum_lo_ahead, sum_lo_back)
    sum_lo_far = send(row(lo, 2), Z_BACK)
    up_one, up_three = pick(row(up, 1), row(up, 3))
    lo_one, lo_three = pick(row(lo, 1), row(lo, 3))
    sum_up_back = send(up_three, Y_AHEAD)
    sum_up_far = wait(sum_up_far)
    sum_lo_back = send(lo_three, Z_AHEAD)
    sum_lo_far = wait(sum_lo_far)
    sum_up_ahead = send(add(up_one, sum_up_far), Y_BACK)
    sum_up_back = wait(sum_up_back)
    sum_lo_ahead = send(add(lo_one, sum_lo_far), Z_BACK)
    sum_lo_back = wait(sum_lo_back)
    sum_up_ahead, sum_lo_ahead = wait(sum_up_ahead, sum_lo_ahead)
    grad_proj = jnp.concatenate(
        [add(row(up, 0), sum_up_ahead, sum_up_back), add(row(lo, 0), sum_lo_ahead, sum_lo_back)]
    )
    grad_proj = send(grad_proj, SWAP)
    layer_out = add(residual, token_proj)
    grad_heads = local(restored_kernel, heads_out.shape, place, grad_heads)
    return (layer_out, grad_heads, grad_proj)


def solution(mesh):
    fine = Mesh(mesh.devices.reshape(2, 4, 2, 4, 2), AXES)
    tokens, grid = P(AXES, None), P(("yh", "z", "c"), ("x", "yl"))
    return jax.shard_map(
        per_device,
        mesh=fine,
        in_specs=(tokens, tokens, grid, tokens),
        out_specs=(tokens, tokens, grid),
        check_vma=False,
    )
```
